32 devices in a mesh: row: 8 (over z, core), col: 4 (over y, x).
Axes of the slice: x: 2, y: 2, z: 4, core: 2. Of those that a mesh axis runs over, the one named last changes fastest.
Arguments:
- inputs: bfloat16 [128, 16384], P('col', 'row'), may hold values from -6 to 6
- output_gradient: bfloat16 [128, 16384], P('col', 'row'), may hold values from -6 to 6
- gate_matrix: bfloat16 [16384, 26624], P('row', 'col'), may hold values from -0.046875 to 0.046875
- up_matrix: bfloat16 [16384, 26624], P('row', 'col'), may hold values from -0.046875 to 0.046875
- down_matrix: bfloat16 [26624, 16384], P('col', 'row'), may hold values from -0.046875 to 0.046875
- gate_adapter_first: bfloat16 [16384, 512], P('row', 'col'), may hold values from -0.046875 to 0.046875
- gate_adapter_second: bfloat16 [512, 26624], P('row', 'col'), may hold values from -0.25 to 0.25
- up_adapter_first: bfloat16 [16384, 512], P('row', 'col'), may hold values from -0.046875 to 0.046875
- up_adapter_second: bfloat16 [512, 26624], P('row', 'col'), may hold values from -0.25 to 0.25
- down_adapter_first: bfloat16 [26624, 512], P('col', 'row'), may hold values from -0.25 to 0.25
- down_adapter_second: bfloat16 [512, 16384], P('col', 'row'), may hold values from -0.046875 to 0.046875
Outputs:
- input_grad: bfloat16 [128, 16384], P('col', 'row')
- grad_gate_in: float32 [16384, 512], P('row', 'col')
- grad_gate_out: float32 [512, 26624], P('row', 'col')
- grad_up_in: float32 [16384, 512], P('row', 'col')
- grad_up_out: float32 [512, 26624], P('row', 'col')
- grad_down_in: float32 [26624, 512], P('col', 'row')
- grad_down_out: float32 [512, 16384], P('col', 'row')
The draws below stay inside these ranges and needn't reach their ends.
All inputs are finite; a program needn't handle non-finite values.
Results may differ from the reference program's by a relative error of at most 0.0062.
Values may be sent and summed in bfloat16 or wider, within the bound.
A program may use at most 192 MiB of HBM per device.

```python
import jax
import jax.numpy as jnp
from jax import lax

MODEL_WIDTH = 16384
HIDDEN_UNITS = 26624
ADAPTER_RANK = 512
TOKENS = 128


def steps_of(stream_key, shape, shards, least, top_value):
    def one(position, shards_of):
        draws = jax.random.uniform(jax.random.fold_in(jax.random.fold_in(stream_key, 6), position), (shards_of,), jnp.float32, least / len(shards), top_value / len(shards))
        return jnp.repeat(jnp.exp(draws), shape[position] // shards_of).reshape((-1,) + (1,) * (len(shape) - position - 1))

    loudness = one(*shards[0])
    for cut in shards[1:]:
        loudness = loudness * one(*cut)
    return loudness


def centred(own_key, extent, deviation, most, split=(), held_as=jnp.bfloat16):
    values = deviation * jax.random.normal(own_key, extent, jnp.float32)
    if split:
        values = values * steps_of(own_key, extent, split, -0.22, 0.18)
    return jnp.clip(values, -most, most).astype(held_as)


def setup_inputs(seed: int = 0) -> dict:
    seeds = jax.random.split(jax.random.key(seed), 12)
    inputs = centred(seeds[0], (TOKENS, MODEL_WIDTH), 1.0, 6.0, ((0, 4), (1, 8)))
    output_gradient = centred(seeds[1], (TOKENS, MODEL_WIDTH), 1.0, 6.0, ((0, 4), (1, 8)))
    gate_matrix = centred(seeds[2], (MODEL_WIDTH, HIDDEN_UNITS), MODEL_WIDTH ** -0.5, 0.046875, ((0, 8), (1, 4)))
    up_matrix = centred(seeds[3], (MODEL_WIDTH, HIDDEN_UNITS), MODEL_WIDTH ** -0.5, 0.046875, ((0, 8), (1, 4)))
    down_matrix = centred(seeds[4], (HIDDEN_UNITS, MODEL_WIDTH), MODEL_WIDTH ** -0.5, 0.046875, ((0, 4), (1, 8)))
    gate_adapter_first = centred(seeds[5], (MODEL_WIDTH, ADAPTER_RANK), MODEL_WIDTH ** -0.5, 0.046875, ((0, 8), (1, 4)))
    gate_adapter_second = centred(seeds[6], (ADAPTER_RANK, HIDDEN_UNITS), ADAPTER_RANK ** -0.5, 0.25, ((0, 8), (1, 4)))
    up_adapter_first = centred(seeds[7], (MODEL_WIDTH, ADAPTER_RANK), MODEL_WIDTH ** -0.5, 0.046875, ((0, 8), (1, 4)))
    up_adapter_second = centred(seeds[8], (ADAPTER_RANK, HIDDEN_UNITS), ADAPTER_RANK ** -0.5, 0.25, ((0, 8), (1, 4)))
    down_adapter_first = centred(seeds[9], (HIDDEN_UNITS, ADAPTER_RANK), ADAPTER_RANK ** -0.5, 0.25, ((0, 4), (1, 8)))
    down_adapter_second = centred(seeds[10], (ADAPTER_RANK, MODEL_WIDTH), MODEL_WIDTH ** -0.5, 0.046875, ((0, 4), (1, 8)))
    return {"inputs": inputs, "output_gradient": output_gradient, "gate_matrix": gate_matrix, "up_matrix": up_matrix, "down_matrix": down_matrix, "gate_adapter_first": gate_adapter_first, "gate_adapter_second": gate_adapter_second, "up_adapter_first": up_adapter_first, "up_adapter_second": up_adapter_second, "down_adapter_first": down_adapter_first, "down_adapter_second": down_adapter_second}


def matrix_product(first_mat, second_mat):
    return jnp.dot(first_mat, second_mat, preferred_element_type=jnp.float32)


def product_transposed(first_mat, second_mat):
    return lax.dot_general(first_mat, second_mat, (((1,), (1,)), ((), ())), preferred_element_type=jnp.float32)


def product_tn(first_mat, second_mat):
    return lax.dot_general(first_mat, second_mat, (((0,), (0,)), ((), ())), preferred_element_type=jnp.float32)


def gated_back(gate_pre, up_pre, hid_grad):
    sigmoid_g = jax.nn.sigmoid(gate_pre)
    silu_g = gate_pre * sigmoid_g
    hidden_state = (silu_g * up_pre).astype(jnp.bfloat16)
    gate_gradient = (hid_grad * up_pre * sigmoid_g * (1.0 + gate_pre * (1.0 - sigmoid_g))).astype(jnp.bfloat16)
    up_gradient = (hid_grad * silu_g).astype(jnp.bfloat16)
    return hidden_state, gate_gradient, up_gradient


def reference(inputs, output_gradient, gate_matrix, up_matrix, down_matrix, gate_adapter_first, gate_adapter_second, up_adapter_first, up_adapter_second, down_adapter_first, down_adapter_second):
    reduced_gate = matrix_product(inputs, gate_adapter_first).astype(jnp.bfloat16)
    reduced_up = matrix_product(inputs, up_adapter_first).astype(jnp.bfloat16)
    reduced_cotangent = product_transposed(output_gradient, down_adapter_second).astype(jnp.bfloat16)
    gate_pre = matrix_product(inputs, gate_matrix) + matrix_product(reduced_gate, gate_adapter_second)
    up_pre = matrix_product(inputs, up_matrix) + matrix_product(reduced_up, up_adapter_second)
    hid_grad = product_transposed(output_gradient, down_matrix) + product_transposed(reduced_cotangent, down_adapter_first)
    hidden_state, gate_gradient, up_gradient = gated_back(gate_pre, up_pre, hid_grad)
    gate_reduced_gradient = product_transposed(gate_gradient, gate_adapter_second).astype(jnp.bfloat16)
    up_reduced_gradient = product_transposed(up_gradient, up_adapter_second).astype(jnp.bfloat16)
    hidden_reduced = matrix_product(hidden_state, down_adapter_first).astype(jnp.bfloat16)
    total = product_transposed(gate_gradient, gate_matrix) + product_transposed(up_gradient, up_matrix)
    total = total + product_transposed(gate_reduced_gradient, gate_adapter_first) + product_transposed(up_reduced_gradient, up_adapter_first)
    input_grad = total.astype(jnp.bfloat16)
    grad_gate_in = product_tn(inputs, gate_reduced_gradient)
    grad_gate_out = product_tn(reduced_gate, gate_gradient)
    grad_up_in = product_tn(inputs, up_reduced_gradient)
    grad_up_out = product_tn(reduced_up, up_gradient)
    grad_down_in = product_tn(hidden_state, reduced_cotangent)
    grad_down_out = product_tn(hidden_reduced, output_gradient)
    return (input_grad, grad_gate_in, grad_gate_out, grad_up_in, grad_up_out, grad_down_in, grad_down_out)
```

```python
import jax
import jax.numpy as jnp
from jax import lax
from jax.sharding import PartitionSpec as P


CHUNKS = 4


def matrix_product(first_mat, second_mat):
    return jnp.dot(first_mat, second_mat, preferred_element_type=jnp.float32)


def product_transposed(first_mat, second_mat):
    return lax.dot_general(
        first_mat, second_mat, (((1,), (1,)), ((), ())), preferred_element_type=jnp.float32
    )


def product_tn(first_mat, second_mat):
    return lax.dot_general(
        first_mat, second_mat, (((0,), (0,)), ((), ())), preferred_element_type=jnp.float32
    )


def gated_back(gate_pre, up_pre, hid_grad):
    sigmoid_g = jax.nn.sigmoid(gate_pre)
    silu_g = gate_pre * sigmoid_g
    hidden_state = (silu_g * up_pre).astype(jnp.bfloat16)
    gate_gradient = (hid_grad * up_pre * sigmoid_g * (1.0 + gate_pre * (1.0 - sigmoid_g))).astype(
        jnp.bfloat16
    )
    up_gradient = (hid_grad * silu_g).astype(jnp.bfloat16)
    return (hidden_state, gate_gradient, up_gradient)


def swap(value, axis, bit):
    count = lax.axis_size(axis)
    return lax.ppermute(value, axis, [(one, one ^ bit) for one in range(count)])


def sum_halves(value, axis, bits):
    index = lax.axis_index(axis)
    for bit in bits:
        half = value.shape[0] // 2
        upper = (index // bit) % 2
        sent = lax.dynamic_slice_in_dim(value, (1 - upper) * half, half, 0)
        kept = lax.dynamic_slice_in_dim(value, upper * half, half, 0)
        value = kept + swap(sent.astype(jnp.bfloat16), axis, bit).astype(jnp.float32)
    return value


def join_halves(value, axis, bits):
    index = lax.axis_index(axis)
    for bit in reversed(bits):
        upper = (index // bit) % 2 == 1
        other = swap(value, axis, bit)
        value = jnp.concatenate(
            (jnp.where(upper, other, value), jnp.where(upper, value, other)), axis=0
        )
    return value


def bits_of(axis):
    count = lax.axis_size(axis)
    return [1 << place for place in range(count.bit_length() - 1)]


def on_device(
    inputs,
    output_gradient,
    gate_matrix,
    up_matrix,
    down_matrix,
    gate_adapter_first,
    gate_adapter_second,
    up_adapter_first,
    up_adapter_second,
    down_adapter_first,
    down_adapter_second,
):
    row_index = lax.axis_index("row")
    col_index = lax.axis_index("col")
    row_bits = bits_of("row")
    col_bits = bits_of("col")[::-1]
    width = inputs.shape[1]
    both = join_halves(jnp.concatenate((inputs, output_gradient), axis=1), "col", col_bits)
    x, dy = both[:, :width], both[:, width:]
    rank_column = gate_adapter_first.shape[1]
    rank_row = gate_adapter_second.shape[0]
    units = gate_matrix.shape[1]
    chunks = CHUNKS if units % (CHUNKS * 128) == 0 else 1
    piece = units // chunks

    low = jnp.stack(
        (
            matrix_product(x, gate_adapter_first),
            matrix_product(x, up_adapter_first),
            product_transposed(dy, down_adapter_second),
        )
    )
    low = lax.psum(low, "row").astype(jnp.bfloat16)
    low = lax.all_gather(low, "col", axis=2, tiled=True)
    low = lax.dynamic_slice_in_dim(low, row_index * rank_row, rank_row, 2)
    low_gate, low_up, low_back = low[0], low[1], low[2]

    hidden_parts, gate_parts, up_parts = [], [], []
    for step in range(chunks):
        cut = slice(step * piece, (step + 1) * piece)
        gate_portion = matrix_product(x, gate_matrix[:, cut]) + matrix_product(
            low_gate, gate_adapter_second[:, cut]
        )
        up_portion = matrix_product(x, up_matrix[:, cut]) + matrix_product(
            low_up, up_adapter_second[:, cut]
        )
        back_portion = product_transposed(dy, down_matrix[cut]) + product_transposed(
            low_back, down_adapter_first[cut]
        )
        total = sum_halves(
            jnp.concatenate((gate_portion, up_portion, back_portion), axis=1), "row", row_bits
        )
        made = gated_back(
            total[:, :piece], total[:, piece : 2 * piece], total[:, 2 * piece :]
        )
        full = join_halves(jnp.concatenate(made, axis=1), "row", row_bits)
        hidden_parts.append(full[:, :piece])
        gate_parts.append(full[:, piece : 2 * piece])
        up_parts.append(full[:, 2 * piece :])

    input_portion = 0.0
    low_grads = 0.0
    out_gate, out_up, in_down = [], [], []
    for step in range(chunks):
        cut = slice(step * piece, (step + 1) * piece)
        hidden, gate_grad, up_grad = hidden_parts[step], gate_parts[step], up_parts[step]
        low_grads = low_grads + jnp.stack(
            (
                product_transposed(gate_grad, gate_adapter_second[:, cut]),
                product_transposed(up_grad, up_adapter_second[:, cut]),
                matrix_product(hidden, down_adapter_first[cut]),
            )
        )
        input_portion = (
            input_portion
            + product_transposed(gate_grad, gate_matrix[:, cut])
            + product_transposed(up_grad, up_matrix[:, cut])
        )
        out_gate.append(product_tn(low_gate, gate_grad))
        out_up.append(product_tn(low_up, up_grad))
        in_down.append(product_tn(hidden, low_back))

    low_grads = lax.psum(low_grads, "col").astype(jnp.bfloat16)
    low_grads = lax.all_gather(low_grads, "row", axis=2, tiled=True)
    low_grads = lax.dynamic_slice_in_dim(low_grads, col_index * rank_column, rank_column, 2)
    gate_low, up_low, hidden_low = low_grads[0], low_grads[1], low_grads[2]
    input_portion = (
        input_portion
        + product_transposed(gate_low, gate_adapter_first)
        + product_transposed(up_low, up_adapter_first)
    )
    input_grad = sum_halves(input_portion, "col", col_bits).astype(jnp.bfloat16)
    return (
        input_grad,
        product_tn(x, gate_low),
        jnp.concatenate(out_gate, axis=1),
        product_tn(x, up_low),
        jnp.concatenate(out_up, axis=1),
        jnp.concatenate(in_down, axis=0),
        product_tn(hidden_low, dy),
    )


def solution(mesh):
    return jax.shard_map(
        on_device,
        mesh=mesh,
        in_specs=(
            P("col", "row"),
            P("col", "row"),
            P("row", "col"),
            P("row", "col"),
            P("col", "row"),
            P("row", "col"),
            P("row", "col"),
            P("row", "col"),
            P("row", "col"),
            P("col", "row"),
            P("col", "row"),
        ),
        out_specs=(
            P("col", "row"),
            P("row", "col"),
            P("row", "col"),
            P("row", "col"),
            P("row", "col"),
            P("col", "row"),
            P("col", "row"),
        ),
        check_vma=False,
    )
```
